1024 devices in a mesh: row: 32 (over x, z_hi, core), col: 32 (over y, z_lo).
Axes of the slice: x: 8, y: 8, z: 8 (z_hi: 2, z_lo: 4; z = z_hi * 4 + z_lo), core: 2. Of those that a mesh axis runs over, the one named last changes fastest.
Arguments:
- images: bfloat16 [393216, 1152], P(('row', 'col')), may hold values from -0.1875 to 0.1875
- texts: bfloat16 [393216, 1152], P(('row', 'col')), may hold values from -0.1875 to 0.1875
- labels: int32 [1024, 384], P(('row', 'col')), may hold values from 0 to 383, each once within a row
- logit_scale: float32 [1], replicated, may hold values from 4 to 16
- logit_bias: float32 [1], replicated, may hold values from -3 to -1
Outputs:
- row_loss: float32 [393216], P(('row', 'col'))
- image_grad: bfloat16 [393216, 1152], P(('row', 'col'))
- text_grad: bfloat16 [393216, 1152], P(('row', 'col'))
The draws below stay inside these ranges and needn't reach their ends.
Inputs may be any that keep to these rules, and one draw needn't show every extreme that they name: Each row of labels is a permutation of 0 to 383.
All inputs are finite; a program needn't handle non-finite values.
Results may differ from the reference program's by a relative error of at most 0.0064.
Values may be sent and summed in bfloat16 or wider, within the bound.
No kernel may reach another device: no remote copies, remote signals or barrier semaphores. Data moves between devices by JAX's collectives and lax.ppermute only.
A program may use at most 32 MiB of HBM per device.

```python
import math
import jax
import jax.numpy as jnp
from jax import lax

D = 1152
B = 384
ROWS = 393216
BLOCKS = 1024
N_ROW = 32
N_COL = 32


def shard_levels(own_key, shape, split, low, largest):
    level, own = 1.0, jax.random.fold_in(own_key, 6)
    for axis_at, parts in split:
        steps = jnp.exp(jax.random.uniform(jax.random.fold_in(own, axis_at), (parts,), jnp.float32, low / len(split), largest / len(split)))
        level = level * jnp.repeat(steps, shape[axis_at] // parts).reshape([-1 if axis == axis_at else 1 for axis in range(len(shape))])
    return level


def centred(key, extent, deviation, reach, cuts=(), held_as=jnp.bfloat16):
    result = deviation * jax.random.normal(key, extent, jnp.float32)
    if cuts:
        result = result * shard_levels(key, extent, cuts, -0.22, 0.18)
    return jnp.clip(result, -reach, reach).astype(held_as)


def setup_inputs(seed: int = 0) -> dict:
    arg_keys = jax.random.split(jax.random.key(seed), 6)
    images = centred(arg_keys[0], (ROWS, D), D ** -0.5, 0.1875, ((0, 1024),))
    texts = centred(arg_keys[1], (ROWS, D), D ** -0.5, 0.1875, ((0, 1024),))
    labels = jax.vmap(lambda own: jax.random.permutation(own, B))(jax.random.split(arg_keys[2], BLOCKS)).reshape((BLOCKS, B)).astype(jnp.int32)
    logit_scale = jnp.clip(jnp.exp(jax.random.uniform(arg_keys[3], (1,), jnp.float32, math.log(4.0), math.log(16.0))), 4.0, 16.0)
    logit_bias = jnp.clip(jax.random.uniform(arg_keys[4], (1,), jnp.float32, -3.0, -1.0), -3.0, -1.0)
    return dict(images=images, texts=texts, labels=labels, logit_scale=logit_scale, logit_bias=logit_bias)


def unit_rows(raw):
    values = raw.astype(jnp.float32)
    inv = lax.rsqrt(lax.optimization_barrier(jnp.sum(values * values, axis=-1, keepdims=True)) + 1e-06)
    return ((values * inv).astype(jnp.bfloat16), inv)

def score_block(left, right, scale, bias, signs):
    logits = jnp.dot(left, right.T, preferred_element_type=jnp.float32) * scale + bias
    terms = jax.nn.softplus(-signs * logits)
    weight = (-scale * signs * jax.nn.sigmoid(-signs * logits)).astype(jnp.bfloat16)
    return (lax.optimization_barrier(jnp.sum(terms, axis=1)), weight)

def back_rows(raw, inv, unit_grad):
    values = raw.astype(jnp.float32)
    inner = lax.optimization_barrier(jnp.sum(values * unit_grad, axis=-1, keepdims=True))
    return (inv * unit_grad - inv * inv * inv * values * inner).astype(jnp.bfloat16)

def transposed(weight, other):
    return lax.dot_general(weight, other, (((0,), (0,)), ((), ())), preferred_element_type=jnp.float32)

def reference(images, texts, labels, logit_scale, logit_bias):
    rows_per = labels.shape[1]
    width = images.shape[1]
    count = labels.shape[0]
    image_blocks = images.reshape(count, rows_per, width)
    text_blocks = texts.reshape(count, rows_per, width)
    scale = logit_scale[0]
    bias = logit_bias[0]
    column_ids = jnp.arange(rows_per, dtype=jnp.int32)

    def one_block(index):
        row_idx = index // N_COL
        col_idx = index % N_COL
        row_mate = jnp.bitwise_xor(row_idx, N_ROW // 2) * N_COL + col_idx
        col_mate = row_idx * N_COL + jnp.bitwise_xor(col_idx, N_COL // 2)
        image_unit, image_inv = unit_rows(image_blocks[index])
        text_unit, text_inv = unit_rows(text_blocks[index])
        row_image, unused_a = unit_rows(image_blocks[row_mate])
        row_text, unused_b = unit_rows(text_blocks[row_mate])
        col_image, unused_c = unit_rows(image_blocks[col_mate])
        col_text, unused_d = unit_rows(text_blocks[col_mate])
        own_sign = jnp.where(labels[index][:, None] == column_ids[None, :], 1.0, -1.0).astype(jnp.float32)
        loss_own, weight_own = score_block(image_unit, text_unit, scale, bias, own_sign)
        loss_row, weight_row = score_block(image_unit, row_text, scale, bias, -1.0)
        loss_col, weight_col = score_block(image_unit, col_text, scale, bias, -1.0)
        unused_e, weight_in_row = score_block(row_image, text_unit, scale, bias, -1.0)
        unused_f, weight_in_col = score_block(col_image, text_unit, scale, bias, -1.0)
        image_unit_grad = jnp.dot(weight_own, text_unit, preferred_element_type=jnp.float32) + jnp.dot(weight_row, row_text, preferred_element_type=jnp.float32) + jnp.dot(weight_col, col_text, preferred_element_type=jnp.float32)
        part_row = transposed(weight_in_row, row_image).astype(jnp.bfloat16)
        part_col = transposed(weight_in_col, col_image).astype(jnp.bfloat16)
        text_unit_grad = transposed(weight_own, image_unit) + part_row.astype(jnp.float32) + part_col.astype(jnp.float32)
        row_loss = (loss_own + loss_row + loss_col) / (3.0 * rows_per)
        image_grad = back_rows(image_blocks[index], image_inv, image_unit_grad)
        text_grad = back_rows(text_blocks[index], text_inv, text_unit_grad)
        return (row_loss, image_grad, text_grad)
    row_loss, image_grad, text_grad = lax.map(one_block, jnp.arange(count, dtype=jnp.int32))
    return (row_loss.reshape(count * rows_per), image_grad.reshape(count * rows_per, width), text_grad.reshape(count * rows_per, width))
```

```python
import functools
import jax
import jax.numpy as jnp
from jax import lax
from jax.experimental import pallas as pl
from jax.experimental.pallas import tpu as pltpu
from jax.sharding import PartitionSpec as P


def from_partner(block, axis):
    count = lax.axis_size(axis)
    half = count // 2
    return lax.ppermute(block, axis, [(at, at ^ half) for at in range(count)])


def unit_rows(raw):
    values = raw.astype(jnp.float32)
    inv = lax.rsqrt(jnp.sum(values * values, axis=-1, keepdims=True) + 1e-06)
    return ((values * inv).astype(jnp.bfloat16), inv)


def score_block(left, right, scale, bias, signs):
    logits = jnp.dot(left, right.T, preferred_element_type=jnp.float32) * scale + bias
    terms = jax.nn.softplus(-signs * logits)
    weight = (-scale * signs * jax.nn.sigmoid(-signs * logits)).astype(jnp.bfloat16)
    return (jnp.sum(terms, axis=1), weight)


def back_rows(raw, inv, unit_grad):
    values = raw.astype(jnp.float32)
    inner = jnp.sum(values * unit_grad, axis=-1, keepdims=True)
    return (inv * unit_grad - inv * inv * inv * values * inner).astype(jnp.bfloat16)


def transposed(weight, other):
    return lax.dot_general(
        weight, other, (((0,), (0,)), ((), ())), preferred_element_type=jnp.float32
    )


def cross_part(scale_ref, bias_ref, raw_ref, text_unit):
    scale = scale_ref[0]
    bias = bias_ref[0]
    unit, _ = unit_rows(raw_ref[...])
    dots = lax.dot_general(
        text_unit, unit, (((1,), (1,)), ((), ())), preferred_element_type=jnp.float32
    )
    weight = (scale * jax.nn.sigmoid(dots * scale + bias)).astype(jnp.bfloat16)
    return jnp.dot(weight, unit, preferred_element_type=jnp.float32)


def add_part(scale_ref, bias_ref, raw_ref, unit_ref, total_ref, out_ref):
    out_ref[...] = total_ref[...] + cross_part(scale_ref, bias_ref, raw_ref, unit_ref[...])


def add_last(scale_ref, bias_ref, raw_ref, unit_ref, total_ref, text_ref, inv_ref, out_ref):
    grad = total_ref[...] + cross_part(scale_ref, bias_ref, raw_ref, unit_ref[...])
    out_ref[...] = back_rows(text_ref[...], inv_ref[...], grad)


def call(kernel, out, *args):
    smem = pl.BlockSpec(memory_space=pltpu.SMEM)
    vmem = pl.BlockSpec(memory_space=pltpu.VMEM)
    rows, width = out.shape
    return pl.pallas_call(
        kernel,
        out_shape=out,
        in_specs=[smem, smem] + [vmem] * (len(args) - 2),
        out_specs=vmem,
        compiler_params=pltpu.CompilerParams(vmem_limit_bytes=40 * 1024 * 1024),
        cost_estimate=pl.CostEstimate(
            flops=4 * rows * rows * width,
            bytes_accessed=12 * rows * width,
            transcendentals=2 * rows * rows,
        ),
    )(*args)


def per_device(images, texts, labels, logit_scale, logit_bias):
    rows_per, width = images.shape
    scale = logit_scale[0]
    bias = logit_bias[0]
    row_text = from_partner(texts, "row")
    col_text = from_partner(texts, "col")
    row_image = from_partner(images, "row")
    col_image = from_partner(images, "col")

    image_unit, image_inv = unit_rows(images)
    text_unit, text_inv = unit_rows(texts)
    column_ids = jnp.arange(rows_per, dtype=jnp.int32)
    own_sign = jnp.where(labels[0][:, None] == column_ids[None, :], 1.0, -1.0).astype(jnp.float32)
    loss_own, weight_own = score_block(image_unit, text_unit, scale, bias, own_sign)
    text_total = transposed(weight_own, image_unit)

    row_unit, _ = unit_rows(row_text)
    loss_row, weight_row = score_block(image_unit, row_unit, scale, bias, -1.0)
    col_unit, _ = unit_rows(col_text)
    loss_col, weight_col = score_block(image_unit, col_unit, scale, bias, -1.0)
    image_unit_grad = (
        jnp.dot(weight_own, text_unit, preferred_element_type=jnp.float32)
        + jnp.dot(weight_row, row_unit, preferred_element_type=jnp.float32)
        + jnp.dot(weight_col, col_unit, preferred_element_type=jnp.float32)
    )
    row_loss = (loss_own + loss_row + loss_col) / (3.0 * rows_per)
    image_grad = back_rows(images, image_inv, image_unit_grad)

    wide = jax.ShapeDtypeStruct((rows_per, width), jnp.float32)
    half = jax.ShapeDtypeStruct((rows_per, width), jnp.bfloat16)
    text_total = call(add_part, wide, logit_scale, logit_bias, row_image, text_unit, text_total)
    text_grad = call(
        add_last, half, logit_scale, logit_bias, col_image, text_unit, text_total, texts, text_inv
    )
    return (row_loss, image_grad, text_grad)


def solution(mesh):
    placed = (P(("row", "col"), None), P(("row", "col"), None), P(("row", "col"), None), P(), P())
    return jax.shard_map(
        per_device,
        mesh=mesh,
        in_specs=placed,
        out_specs=(P(("row", "col")), P(("row", "col"), None), P(("row", "col"), None)),
        check_vma=False,
    )
```

```python
import functools
import jax
import jax.numpy as jnp
from jax import lax
from jax.experimental import pallas as pl
from jax.experimental.pallas import tpu as pltpu
from jax.sharding import PartitionSpec as P


def from_partner(block, axis):
    count = lax.axis_size(axis)
    half = count // 2
    return lax.ppermute(block, axis, [(at, at ^ half) for at in range(count)])


def unit_rows(raw):
    values = raw.astype(jnp.float32)
    inv = lax.rsqrt(jnp.sum(values * values, axis=-1, keepdims=True) + 1e-06)
    return ((values * inv).astype(jnp.bfloat16), inv)


def score_block(left, right, scale, bias, signs):
    logits = jnp.dot(left, right.T, preferred_element_type=jnp.float32) * scale + bias
    terms = jax.nn.softplus(-signs * logits)
    weight = (-scale * signs * jax.nn.sigmoid(-signs * logits)).astype(jnp.bfloat16)
    return (jnp.sum(terms, axis=1), weight)


def back_rows(raw, inv, unit_grad):
    values = raw.astype(jnp.float32)
    inner = jnp.sum(values * unit_grad, axis=-1, keepdims=True)
    return (inv * unit_grad - inv * inv * inv * values * inner).astype(jnp.bfloat16)


def transposed(weight, other):
    return lax.dot_general(
        weight, other, (((0,), (0,)), ((), ())), preferred_element_type=jnp.float32
    )


def cross_part(scale_ref, bias_ref, raw_ref, text_unit):
    scale = scale_ref[0]
    bias = bias_ref[0]
    unit, _ = unit_rows(raw_ref[...])
    dots = lax.dot_general(
        text_unit, unit, (((1,), (1,)), ((), ())), preferred_element_type=jnp.float32
    )
    weight = (scale * jax.nn.sigmoid(dots * scale + bias)).astype(jnp.bfloat16)
    return jnp.dot(weight, unit, preferred_element_type=jnp.float32)


def add_part(scale_ref, bias_ref, raw_ref, unit_ref, total_ref, out_ref):
    out_ref[...] = total_ref[...] + cross_part(scale_ref, bias_ref, raw_ref, unit_ref[...])


def add_last(scale_ref, bias_ref, raw_ref, unit_ref, total_ref, text_ref, inv_ref, out_ref):
    grad = total_ref[...] + cross_part(scale_ref, bias_ref, raw_ref, unit_ref[...])
    out_ref[...] = back_rows(text_ref[...], inv_ref[...], grad)


def call(kernel, out, *args):
    smem = pl.BlockSpec(memory_space=pltpu.SMEM)
    vmem = pl.BlockSpec(memory_space=pltpu.VMEM)
    rows, width = out.shape
    return pl.pallas_call(
        kernel,
        out_shape=out,
        in_specs=[smem, smem] + [vmem] * (len(args) - 2),
        out_specs=vmem,
        compiler_params=pltpu.CompilerParams(vmem_limit_bytes=40 * 1024 * 1024),
        cost_estimate=pl.CostEstimate(
            flops=4 * rows * rows * width,
            bytes_accessed=12 * rows * width,
            transcendentals=2 * rows * rows,
        ),
    )(*args)


def per_device(images, texts, labels, logit_scale, logit_bias):
    rows_per, width = images.shape
    scale = logit_scale[0]
    bias = logit_bias[0]
    col_text = from_partner(texts, "col")
    row_text = from_partner(texts, "row")
    col_image = from_partner(images, "col")
    row_image = from_partner(images, "row")

    image_unit, image_inv = unit_rows(images)
    text_unit, text_inv = unit_rows(texts)
    column_ids = jnp.arange(rows_per, dtype=jnp.int32)
    own_sign = jnp.where(labels[0][:, None] == column_ids[None, :], 1.0, -1.0).astype(jnp.float32)
    loss_own, weight_own = score_block(image_unit, text_unit, scale, bias, own_sign)
    text_total = transposed(weight_own, image_unit)

    col_unit, _ = unit_rows(col_text)
    loss_col, weight_col = score_block(image_unit, col_unit, scale, bias, -1.0)
    row_unit, _ = unit_rows(row_text)
    loss_row, weight_row = score_block(image_unit, row_unit, scale, bias, -1.0)
    image_unit_grad = (
        jnp.dot(weight_own, text_unit, preferred_element_type=jnp.float32)
        + jnp.dot(weight_row, row_unit, preferred_element_type=jnp.float32)
        + jnp.dot(weight_col, col_unit, preferred_element_type=jnp.float32)
    )
    row_loss = (loss_own + loss_row + loss_col) / (3.0 * rows_per)
    image_grad = back_rows(images, image_inv, image_unit_grad)

    wide = jax.ShapeDtypeStruct((rows_per, width), jnp.float32)
    half = jax.ShapeDtypeStruct((rows_per, width), jnp.bfloat16)
    text_total = call(add_part, wide, logit_scale, logit_bias, col_image, text_unit, text_total)
    text_grad = call(
        add_last, half, logit_scale, logit_bias, row_image, text_unit, text_total, texts, text_inv
    )
    return (row_loss, image_grad, text_grad)


def solution(mesh):
    placed = (P(("row", "col"), None), P(("row", "col"), None), P(("row", "col"), None), P(), P())
    return jax.shard_map(
        per_device,
        mesh=mesh,
        in_specs=placed,
        out_specs=(P(("row", "col")), P(("row", "col"), None), P(("row", "col"), None)),
        check_vma=False,
    )
```

```python
import functools
import jax
import jax.numpy as jnp
from jax import lax
from jax.experimental import pallas as pl
from jax.experimental.pallas import tpu as pltpu
from jax.sharding import PartitionSpec as P

STEP = 128


def from_partner(block, axis):
    count = lax.axis_size(axis)
    half = count // 2
    return lax.ppermute(block, axis, [(at, at ^ half) for at in range(count)])


def unit_rows(raw):
    values = raw.astype(jnp.float32)
    inv = lax.rsqrt(jnp.sum(values * values, axis=-1, keepdims=True) + 1e-06)
    return ((values * inv).astype(jnp.bfloat16), inv)


def score_block(left, right, scale, bias, signs):
    logits = jnp.dot(left, right.T, preferred_element_type=jnp.float32) * scale + bias
    terms = jax.nn.softplus(-signs * logits)
    weight = (-scale * signs * jax.nn.sigmoid(-signs * logits)).astype(jnp.bfloat16)
    return (jnp.sum(terms, axis=1), weight)


def back_rows(raw, inv, unit_grad):
    values = raw.astype(jnp.float32)
    inner = jnp.sum(values * unit_grad, axis=-1, keepdims=True)
    return (inv * unit_grad - inv * inv * inv * values * inner).astype(jnp.bfloat16)


def transposed(weight, other):
    return lax.dot_general(
        weight, other, (((0,), (0,)), ((), ())), preferred_element_type=jnp.float32
    )


def plain_weight(dots, scale, bias):
    logits = dots * scale + bias
    return ((scale * jax.nn.sigmoid(logits)).astype(jnp.bfloat16), logits)


def dot_rows(left, right):
    return lax.dot_general(
        left, right, (((1,), (1,)), ((), ())), preferred_element_type=jnp.float32
    )


def image_side(last, scale_ref, bias_ref, raw_ref, unit_ref, loss_ref, total_ref, *rest):
    loss_out, grad_out, other = rest[-3:]
    other[...] = unit_rows(raw_ref[...])[0]
    scale = scale_ref[0]
    bias = bias_ref[0]
    for at in range(0, raw_ref.shape[0], STEP):
        rows = pl.ds(at, STEP)
        weight, logits = plain_weight(dot_rows(unit_ref[rows, :], other[...]), scale, bias)
        terms = jnp.maximum(logits, 0.0) + jnp.log1p(jnp.exp(-jnp.abs(logits)))
        loss = loss_ref[rows, :] + jnp.sum(terms, axis=1, keepdims=True)
        grad = total_ref[rows, :] + jnp.dot(
            weight, other[...], preferred_element_type=jnp.float32
        )
        if last:
            image_ref, inv_ref = rest[:2]
            loss_out[rows, :] = loss / (3.0 * raw_ref.shape[0])
            grad_out[rows, :] = back_rows(image_ref[rows, :], inv_ref[rows, :], grad)
        else:
            loss_out[rows, :] = loss
            grad_out[rows, :] = grad


def text_side(scale_ref, bias_ref, raw_ref, unit_ref, total_ref, out_ref, other):
    other[...] = unit_rows(raw_ref[...])[0]
    for at in range(0, raw_ref.shape[0], STEP):
        rows = pl.ds(at, STEP)
        weight, _ = plain_weight(
            dot_rows(unit_ref[rows, :], other[...]), scale_ref[0], bias_ref[0]
        )
        out_ref[rows, :] = total_ref[rows, :] + jnp.dot(
            weight, other[...], preferred_element_type=jnp.float32
        )


def text_last(
    scale_ref, bias_ref, raw_ref, unit_ref, total_ref, text_ref, inv_ref, out_ref, other, done, sems
):
    other[...] = unit_rows(raw_ref[...])[0]
    copies = []
    for index, at in enumerate(range(0, raw_ref.shape[0], STEP)):
        rows = pl.ds(at, STEP)
        weight, _ = plain_weight(
            dot_rows(unit_ref[rows, :], other[...]), scale_ref[0], bias_ref[0]
        )
        grad = total_ref[rows, :] + jnp.dot(
            weight, other[...], preferred_element_type=jnp.float32
        )
        done[rows, :] = back_rows(text_ref[rows, :], inv_ref[rows, :], grad)
        copies.append(
            pltpu.make_async_copy(done.at[rows, :], out_ref.at[rows, :], sems.at[index])
        )
        copies[-1].start()
    for copy in copies:
        copy.wait()


def call(kernel, out, out_specs, scratch, rows, width, *args):
    smem = pl.BlockSpec(memory_space=pltpu.SMEM)
    vmem = pl.BlockSpec(memory_space=pltpu.VMEM)
    return pl.pallas_call(
        kernel,
        out_shape=out,
        in_specs=[smem, smem] + [vmem] * (len(args) - 2),
        out_specs=out_specs,
        scratch_shapes=[pltpu.VMEM((rows, width), jnp.bfloat16)] + scratch,
        compiler_params=pltpu.CompilerParams(vmem_limit_bytes=40 * 1024 * 1024),
        cost_estimate=pl.CostEstimate(
            flops=4 * rows * rows * width,
            bytes_accessed=12 * rows * width,
            transcendentals=2 * rows * rows,
        ),
    )(*args)


def per_device(images, texts, labels, logit_scale, logit_bias):
    rows_per, width = images.shape
    scale = logit_scale[0]
    bias = logit_bias[0]
    col_text = from_partner(texts, "col")
    row_text = from_partner(texts, "row")
    image_unit, image_inv = unit_rows(images)
    col_image = from_partner(images, "col")
    row_image = from_partner(images, "row")
    text_unit, text_inv = unit_rows(texts)
    column_ids = jnp.arange(rows_per, dtype=jnp.int32)
    own_sign = jnp.where(labels[0][:, None] == column_ids[None, :], 1.0, -1.0).astype(jnp.float32)
    loss, weight_own = score_block(image_unit, text_unit, scale, bias, own_sign)
    loss = loss[:, None]
    image_total = jnp.dot(weight_own, text_unit, preferred_element_type=jnp.float32)
    text_total = transposed(weight_own, image_unit)

    vmem = pl.BlockSpec(memory_space=pltpu.VMEM)
    wide = jax.ShapeDtypeStruct((rows_per, width), jnp.float32)
    half = jax.ShapeDtypeStruct((rows_per, width), jnp.bfloat16)
    line = jax.ShapeDtypeStruct((rows_per, 1), jnp.float32)
    loss, image_total = call(
        functools.partial(image_side, False), (line, wide), (vmem, vmem), [], rows_per, width,
        logit_scale, logit_bias, col_text, image_unit, loss, image_total,
    )
    loss, image_grad = call(
        functools.partial(image_side, True), (line, half), (vmem, vmem), [], rows_per, width,
        logit_scale, logit_bias, row_text, image_unit, loss, image_total, images, image_inv,
    )
    image_grad, text_total = lax.optimization_barrier((image_grad, text_total))
    text_total = call(
        text_side, wide, vmem, [], rows_per, width,
        logit_scale, logit_bias, col_image, text_unit, text_total,
    )
    text_grad = call(
        text_last, half, pl.BlockSpec(memory_space=pl.ANY),
        [pltpu.VMEM((rows_per, width), jnp.bfloat16), pltpu.SemaphoreType.DMA((rows_per // STEP,))],
        rows_per, width,
        logit_scale, logit_bias, row_image, text_unit, text_total, texts, text_inv,
    )
    return (loss[:, 0], image_grad, text_grad)


def solution(mesh):
    placed = (P(("row", "col"), None), P(("row", "col"), None), P(("row", "col"), None), P(), P())
    return jax.shard_map(
        per_device,
        mesh=mesh,
        in_specs=placed,
        out_specs=(P(("row", "col")), P(("row", "col"), None), P(("row", "col"), None)),
        check_vma=False,
    )
```

```python
import jax
import jax.numpy as jnp
from jax import lax
from jax.experimental import pallas as pl
from jax.experimental.pallas import tpu as pltpu
from jax.sharding import PartitionSpec as P

STEP = 96


def from_partner(block, axis):
    count = lax.axis_size(axis)
    half = count // 2
    return lax.ppermute(block, axis, [(at, at ^ half) for at in range(count)])


def unit_rows(raw):
    values = raw.astype(jnp.float32)
    inv = lax.rsqrt(jnp.sum(values * values, axis=-1, keepdims=True) + 1e-06)
    return ((values * inv).astype(jnp.bfloat16), inv)


def score_block(left, right, scale, bias, signs):
    logits = jnp.dot(left, right.T, preferred_element_type=jnp.float32) * scale + bias
    terms = jax.nn.softplus(-signs * logits)
    weight = (-scale * signs * jax.nn.sigmoid(-signs * logits)).astype(jnp.bfloat16)
    return (jnp.sum(terms, axis=1), weight)


def back_rows(raw, inv, unit_grad):
    values = raw.astype(jnp.float32)
    inner = jnp.sum(values * unit_grad, axis=-1, keepdims=True)
    return (inv * unit_grad - inv * inv * inv * values * inner).astype(jnp.bfloat16)


def transposed(weight, other):
    return lax.dot_general(
        weight, other, (((0,), (0,)), ((), ())), preferred_element_type=jnp.float32
    )


def plain_weight(dots, scale, bias):
    return (scale * jax.nn.sigmoid(dots * scale + bias)).astype(jnp.bfloat16)


def dot_rows(left, right):
    return lax.dot_general(
        left, right, (((1,), (1,)), ((), ())), preferred_element_type=jnp.float32
    )


def cross_part(scale_ref, bias_ref, raw_ref, unit_ref):
    other = unit_rows(raw_ref[...])[0]
    weight = plain_weight(dot_rows(unit_ref[...], other), scale_ref[0], bias_ref[0])
    return jnp.dot(weight, other, preferred_element_type=jnp.float32)


def text_side(scale_ref, bias_ref, raw_ref, unit_ref, total_ref, out_ref):
    out_ref[...] = total_ref[...] + cross_part(scale_ref, bias_ref, raw_ref, unit_ref)


def text_last(
    scale_ref, bias_ref, raw_ref, unit_ref, total_ref, text_ref, inv_ref, out_ref, grad, done, sems
):
    grad[...] = total_ref[...] + cross_part(scale_ref, bias_ref, raw_ref, unit_ref)
    copies = []
    for index, at in enumerate(range(0, grad.shape[0], STEP)):
        rows = pl.ds(at, STEP)
        done[rows, :] = back_rows(text_ref[rows, :], inv_ref[rows, :], grad[rows, :])
        copies.append(
            pltpu.make_async_copy(done.at[rows, :], out_ref.at[rows, :], sems.at[index])
        )
        copies[-1].start()
    for copy in copies:
        copy.wait()


def call(kernel, out, out_specs, scratch, rows, width, *args):
    smem = pl.BlockSpec(memory_space=pltpu.SMEM)
    vmem = pl.BlockSpec(memory_space=pltpu.VMEM)
    return pl.pallas_call(
        kernel,
        out_shape=out,
        in_specs=[smem, smem] + [vmem] * (len(args) - 2),
        out_specs=out_specs,
        scratch_shapes=scratch,
        compiler_params=pltpu.CompilerParams(vmem_limit_bytes=40 * 1024 * 1024),
        cost_estimate=pl.CostEstimate(
            flops=4 * rows * rows * width,
            bytes_accessed=12 * rows * width,
            transcendentals=2 * rows * rows,
        ),
    )(*args)


def per_device(images, texts, labels, logit_scale, logit_bias):
    rows_per, width = images.shape
    scale = logit_scale[0]
    bias = logit_bias[0]
    col_text = from_partner(texts, "col")
    row_text = from_partner(texts, "row")
    image_unit, image_inv = unit_rows(images)
    col_image = from_partner(images, "col")
    row_image = from_partner(images, "row")
    text_unit, text_inv = unit_rows(texts)
    column_ids = jnp.arange(rows_per, dtype=jnp.int32)
    own_sign = jnp.where(labels[0][:, None] == column_ids[None, :], 1.0, -1.0).astype(jnp.float32)
    loss_own, weight_own = score_block(image_unit, text_unit, scale, bias, own_sign)
    text_total = transposed(weight_own, image_unit)

    col_unit, _ = unit_rows(col_text)
    loss_col, weight_col = score_block(image_unit, col_unit, scale, bias, -1.0)
    loss_col, row_text = lax.optimization_barrier((loss_col, row_text))
    row_unit, _ = unit_rows(row_text)
    loss_row, weight_row = score_block(image_unit, row_unit, scale, bias, -1.0)
    image_unit_grad = (
        jnp.dot(weight_own, text_unit, preferred_element_type=jnp.float32)
        + jnp.dot(weight_col, col_unit, preferred_element_type=jnp.float32)
        + jnp.dot(weight_row, row_unit, preferred_element_type=jnp.float32)
    )
    row_loss = (loss_own + loss_row + loss_col) / (3.0 * rows_per)
    image_grad = back_rows(images, image_inv, image_unit_grad)

    vmem = pl.BlockSpec(memory_space=pltpu.VMEM)
    wide = jax.ShapeDtypeStruct((rows_per, width), jnp.float32)
    half = jax.ShapeDtypeStruct((rows_per, width), jnp.bfloat16)
    image_grad, text_total = lax.optimization_barrier((image_grad, text_total))
    text_total = call(
        text_side, wide, vmem, [], rows_per, width,
        logit_scale, logit_bias, col_image, text_unit, text_total,
    )
    text_grad = call(
        text_last, half, pl.BlockSpec(memory_space=pl.ANY),
        [pltpu.VMEM((rows_per, width), jnp.float32), pltpu.VMEM((rows_per, width), jnp.bfloat16),
         pltpu.SemaphoreType.DMA((rows_per // STEP,))],
        rows_per, width,
        logit_scale, logit_bias, row_image, text_unit, text_total, texts, text_inv,
    )
    return (row_loss, image_grad, text_grad)


def solution(mesh):
    placed = (P(("row", "col"), None), P(("row", "col"), None), P(("row", "col"), None), P(), P())
    return jax.shard_map(
        per_device,
        mesh=mesh,
        in_specs=placed,
        out_specs=(P(("row", "col")), P(("row", "col"), None), P(("row", "col"), None)),
        check_vma=False,
    )
```

```python
import jax
import jax.numpy as jnp
from jax import lax
from jax.experimental import pallas as pl
from jax.experimental.pallas import tpu as pltpu
from jax.sharding import PartitionSpec as P

STEP = 128


def from_partner(block, axis):
    count = lax.axis_size(axis)
    half = count // 2
    return lax.ppermute(block, axis, [(at, at ^ half) for at in range(count)])


def unit_rows(raw):
    values = raw.astype(jnp.float32)
    inv = lax.rsqrt(jnp.sum(values * values, axis=-1, keepdims=True) + 1e-06)
    return ((values * inv).astype(jnp.bfloat16), inv)


def score_block(left, right, scale, bias, signs):
    logits = jnp.dot(left, right.T, preferred_element_type=jnp.float32) * scale + bias
    terms = jax.nn.softplus(-signs * logits)
    weight = (-scale * signs * jax.nn.sigmoid(-signs * logits)).astype(jnp.bfloat16)
    return (jnp.sum(terms, axis=1), weight)


def raw_grad(raw, inv, unit_grad):
    values = raw.astype(jnp.float32)
    inner = jnp.sum(values * unit_grad, axis=-1, keepdims=True)
    return inv * unit_grad - inv * inv * inv * values * inner


def back_rows(raw, inv, unit_grad):
    return raw_grad(raw, inv, unit_grad).astype(jnp.bfloat16)


def transposed(weight, other):
    return lax.dot_general(
        weight, other, (((0,), (0,)), ((), ())), preferred_element_type=jnp.float32
    )


def plain_weight(dots, scale, bias):
    return (scale * jax.nn.sigmoid(dots * scale + bias)).astype(jnp.bfloat16)


def dot_rows(left, right):
    return lax.dot_general(
        left, right, (((1,), (1,)), ((), ())), preferred_element_type=jnp.float32
    )


def cross_weight(scale_ref, bias_ref, raw_ref, unit_ref):
    other = unit_rows(raw_ref[...])[0]
    dots = dot_rows(unit_ref[...], other)
    return (other, dots, plain_weight(dots, scale_ref[0], bias_ref[0]))


def text_side(scale_ref, bias_ref, raw_ref, unit_ref, total_ref, text_ref, inv_ref, out_ref):
    other, _, weight = cross_weight(scale_ref, bias_ref, raw_ref, unit_ref)
    grad = total_ref[...] + jnp.dot(weight, other, preferred_element_type=jnp.float32)
    out_ref[...] = raw_grad(text_ref[...], inv_ref[...], grad)


def text_last(
    scale_ref, bias_ref, raw_ref, unit_ref, base_ref, text_ref, inv_ref, out_ref, done, sems
):
    other, dots, weight = cross_weight(scale_ref, bias_ref, raw_ref, unit_ref)
    inv = inv_ref[...]
    inner = jnp.sum(weight.astype(jnp.float32) * dots, axis=1, keepdims=True)
    along = inv * inv * inner
    copies = []
    for index, at in enumerate(range(0, done.shape[0], STEP)):
        rows = pl.ds(at, STEP)
        part = jnp.dot(weight[at : at + STEP], other, preferred_element_type=jnp.float32)
        values = text_ref[rows, :].astype(jnp.float32)
        done[rows, :] = (
            base_ref[rows, :] + inv[at : at + STEP] * part - along[at : at + STEP] * values
        ).astype(jnp.bfloat16)
        copies.append(
            pltpu.make_async_copy(done.at[rows, :], out_ref.at[rows, :], sems.at[index])
        )
        copies[-1].start()
    for copy in copies:
        copy.wait()


def call(kernel, out, out_specs, scratch, rows, width, *args):
    smem = pl.BlockSpec(memory_space=pltpu.SMEM)
    vmem = pl.BlockSpec(memory_space=pltpu.VMEM)
    return pl.pallas_call(
        kernel,
        out_shape=out,
        in_specs=[smem, smem] + [vmem] * (len(args) - 2),
        out_specs=out_specs,
        scratch_shapes=scratch,
        compiler_params=pltpu.CompilerParams(vmem_limit_bytes=40 * 1024 * 1024),
        cost_estimate=pl.CostEstimate(
            flops=4 * rows * rows * width,
            bytes_accessed=12 * rows * width,
            transcendentals=2 * rows * rows,
        ),
    )(*args)


def per_device(images, texts, labels, logit_scale, logit_bias):
    rows_per, width = images.shape
    scale = logit_scale[0]
    bias = logit_bias[0]
    col_text = from_partner(texts, "col")
    row_text = from_partner(texts, "row")
    image_unit, image_inv = unit_rows(images)
    col_image = from_partner(images, "col")
    row_image = from_partner(images, "row")
    text_unit, text_inv = unit_rows(texts)
    column_ids = jnp.arange(rows_per, dtype=jnp.int32)
    own_sign = jnp.where(labels[0][:, None] == column_ids[None, :], 1.0, -1.0).astype(jnp.float32)
    loss_own, weight_own = score_block(image_unit, text_unit, scale, bias, own_sign)
    text_total = transposed(weight_own, image_unit)

    col_unit, _ = unit_rows(col_text)
    loss_col, weight_col = score_block(image_unit, col_unit, scale, bias, -1.0)
    loss_col, row_text = lax.optimization_barrier((loss_col, row_text))
    row_unit, _ = unit_rows(row_text)
    loss_row, weight_row = score_block(image_unit, row_unit, scale, bias, -1.0)
    image_unit_grad = (
        jnp.dot(weight_own, text_unit, preferred_element_type=jnp.float32)
        + jnp.dot(weight_col, col_unit, preferred_element_type=jnp.float32)
        + jnp.dot(weight_row, row_unit, preferred_element_type=jnp.float32)
    )
    row_loss = (loss_own + loss_row + loss_col) / (3.0 * rows_per)
    image_grad = back_rows(images, image_inv, image_unit_grad)

    vmem = pl.BlockSpec(memory_space=pltpu.VMEM)
    wide = jax.ShapeDtypeStruct((rows_per, width), jnp.float32)
    half = jax.ShapeDtypeStruct((rows_per, width), jnp.bfloat16)
    image_grad, text_total = lax.optimization_barrier((image_grad, text_total))
    text_total = call(
        text_side, wide, vmem, [], rows_per, width,
        logit_scale, logit_bias, col_image, text_unit, text_total, texts, text_inv,
    )
    text_grad = call(
        text_last, half, pl.BlockSpec(memory_space=pl.ANY),
        [pltpu.VMEM((rows_per, width), jnp.bfloat16), pltpu.SemaphoreType.DMA((rows_per // STEP,))],
        rows_per, width,
        logit_scale, logit_bias, row_image, text_unit, text_total, texts, text_inv,
    )
    return (row_loss, image_grad, text_grad)


def solution(mesh):
    placed = (P(("row", "col"), None), P(("row", "col"), None), P(("row", "col"), None), P(), P())
    return jax.shard_map(
        per_device,
        mesh=mesh,
        in_specs=placed,
        out_specs=(P(("row", "col")), P(("row", "col"), None), P(("row", "col"), None)),
        check_vma=False,
    )
```

```python
import jax
import jax.numpy as jnp
from jax import lax
from jax.experimental import pallas as pl
from jax.experimental.pallas import tpu as pltpu
from jax.sharding import PartitionSpec as P

STEP = 128


def from_partner(block, axis):
    count = lax.axis_size(axis)
    half = count // 2
    return lax.ppermute(block, axis, [(at, at ^ half) for at in range(count)])


def unit_rows(raw):
    values = raw.astype(jnp.float32)
    inv = lax.rsqrt(jnp.sum(values * values, axis=-1, keepdims=True) + 1e-06)
    return ((values * inv).astype(jnp.bfloat16), inv)


def score_block(left, right, scale, bias, signs):
    logits = jnp.dot(left, right.T, preferred_element_type=jnp.float32) * scale + bias
    terms = jax.nn.softplus(-signs * logits)
    weight = (-scale * signs * jax.nn.sigmoid(-signs * logits)).astype(jnp.bfloat16)
    return (jnp.sum(terms, axis=1), weight)


def raw_grad(raw, inv, unit_grad):
    values = raw.astype(jnp.float32)
    inner = jnp.sum(values * unit_grad, axis=-1, keepdims=True)
    return inv * unit_grad - inv * inv * inv * values * inner


def back_rows(raw, inv, unit_grad):
    return raw_grad(raw, inv, unit_grad).astype(jnp.bfloat16)


def transposed(weight, other):
    return lax.dot_general(
        weight, other, (((0,), (0,)), ((), ())), preferred_element_type=jnp.float32
    )


def plain_weight(dots, scale, bias):
    return scale * jax.nn.sigmoid(dots * scale + bias)


def dot_rows(left, right):
    return lax.dot_general(
        left, right, (((1,), (1,)), ((), ())), preferred_element_type=jnp.float32
    )


def cross_weight(scale_ref, bias_ref, raw_ref, unit_ref):
    other = unit_rows(raw_ref[...])[0]
    dots = dot_rows(unit_ref[...], other)
    return (other, dots, plain_weight(dots, scale_ref[0], bias_ref[0]).astype(jnp.bfloat16))


def text_side(scale_ref, bias_ref, raw_ref, unit_ref, total_ref, text_ref, inv_ref, out_ref):
    other, _, weight = cross_weight(scale_ref, bias_ref, raw_ref, unit_ref)
    grad = total_ref[...] + jnp.dot(weight, other, preferred_element_type=jnp.float32)
    out_ref[...] = raw_grad(text_ref[...], inv_ref[...], grad)


def text_last(
    scale_ref, bias_ref, raw_ref, unit_ref, base_ref, text_ref, inv_ref, out_ref, done, sems
):
    other = raw_ref[...]
    values = other.astype(jnp.float32)
    theirs = lax.rsqrt(jnp.sum(values * values, axis=1) + 1e-06)[None, :]
    dots = dot_rows(unit_ref[...], other) * theirs
    weight = plain_weight(dots, scale_ref[0], bias_ref[0]).astype(jnp.float32)
    inv = inv_ref[...]
    along = inv * inv * jnp.sum(weight * dots, axis=1, keepdims=True)
    weight = (weight * theirs).astype(jnp.bfloat16)
    copies = []
    for index, at in enumerate(range(0, done.shape[0], STEP)):
        rows = pl.ds(at, STEP)
        part = jnp.dot(weight[at : at + STEP], other, preferred_element_type=jnp.float32)
        text = text_ref[rows, :].astype(jnp.float32)
        done[rows, :] = (
            base_ref[rows, :] + inv[at : at + STEP] * part - along[at : at + STEP] * text
        ).astype(jnp.bfloat16)
        copies.append(
            pltpu.make_async_copy(done.at[rows, :], out_ref.at[rows, :], sems.at[index])
        )
        copies[-1].start()
    for copy in copies:
        copy.wait()


def call(kernel, out, out_specs, scratch, rows, width, *args):
    smem = pl.BlockSpec(memory_space=pltpu.SMEM)
    vmem = pl.BlockSpec(memory_space=pltpu.VMEM)
    return pl.pallas_call(
        kernel,
        out_shape=out,
        in_specs=[smem, smem] + [vmem] * (len(args) - 2),
        out_specs=out_specs,
        scratch_shapes=scratch,
        compiler_params=pltpu.CompilerParams(vmem_limit_bytes=40 * 1024 * 1024),
        cost_estimate=pl.CostEstimate(
            flops=4 * rows * rows * width,
            bytes_accessed=12 * rows * width,
            transcendentals=2 * rows * rows,
        ),
    )(*args)


def per_device(images, texts, labels, logit_scale, logit_bias):
    rows_per, width = images.shape
    scale = logit_scale[0]
    bias = logit_bias[0]
    col_text = from_partner(texts, "col")
    row_text = from_partner(texts, "row")
    image_unit, image_inv = unit_rows(images)
    col_image = from_partner(images, "col")
    row_image = from_partner(images, "row")
    text_unit, text_inv = unit_rows(texts)
    column_ids = jnp.arange(rows_per, dtype=jnp.int32)
    own_sign = jnp.where(labels[0][:, None] == column_ids[None, :], 1.0, -1.0).astype(jnp.float32)
    loss_own, weight_own = score_block(image_unit, text_unit, scale, bias, own_sign)
    text_total = transposed(weight_own, image_unit)

    col_unit, _ = unit_rows(col_text)
    loss_col, weight_col = score_block(image_unit, col_unit, scale, bias, -1.0)
    loss_col, row_text = lax.optimization_barrier((loss_col, row_text))
    row_unit, _ = unit_rows(row_text)
    loss_row, weight_row = score_block(image_unit, row_unit, scale, bias, -1.0)
    image_unit_grad = (
        jnp.dot(weight_own, text_unit, preferred_element_type=jnp.float32)
        + jnp.dot(weight_col, col_unit, preferred_element_type=jnp.float32)
        + jnp.dot(weight_row, row_unit, preferred_element_type=jnp.float32)
    )
    row_loss = (loss_own + loss_row + loss_col) / (3.0 * rows_per)
    image_grad = back_rows(images, image_inv, image_unit_grad)

    vmem = pl.BlockSpec(memory_space=pltpu.VMEM)
    wide = jax.ShapeDtypeStruct((rows_per, width), jnp.float32)
    half = jax.ShapeDtypeStruct((rows_per, width), jnp.bfloat16)
    image_grad, text_total = lax.optimization_barrier((image_grad, text_total))
    text_total = call(
        text_side, wide, vmem, [], rows_per, width,
        logit_scale, logit_bias, col_image, text_unit, text_total, texts, text_inv,
    )
    text_grad = call(
        text_last, half, pl.BlockSpec(memory_space=pl.ANY),
        [pltpu.VMEM((rows_per, width), jnp.bfloat16), pltpu.SemaphoreType.DMA((rows_per // STEP,))],
        rows_per, width,
        logit_scale, logit_bias, row_image, text_unit, text_total, texts, text_inv,
    )
    return (row_loss, image_grad, text_grad)


def solution(mesh):
    placed = (P(("row", "col"), None), P(("row", "col"), None), P(("row", "col"), None), P(), P())
    return jax.shard_map(
        per_device,
        mesh=mesh,
        in_specs=placed,
        out_specs=(P(("row", "col")), P(("row", "col"), None), P(("row", "col"), None)),
        check_vma=False,
    )
```

```python
import jax
import jax.numpy as jnp
from jax import lax
from jax.experimental import pallas as pl
from jax.experimental.pallas import tpu as pltpu
from jax.sharding import PartitionSpec as P

STEP = 128


def from_partner(block, axis):
    count = lax.axis_size(axis)
    half = count // 2
    return lax.ppermute(block, axis, [(at, at ^ half) for at in range(count)])


def unit_rows(raw):
    values = raw.astype(jnp.float32)
    inv = lax.rsqrt(jnp.sum(values * values, axis=-1, keepdims=True) + 1e-06)
    return ((values * inv).astype(jnp.bfloat16), inv)


def score_block(left, right, scale, bias, signs):
    logits = jnp.dot(left, right.T, preferred_element_type=jnp.float32) * scale + bias
    terms = jax.nn.softplus(-signs * logits)
    weight = (-scale * signs * jax.nn.sigmoid(-signs * logits)).astype(jnp.bfloat16)
    return (jnp.sum(terms, axis=1), weight)


def raw_grad(raw, inv, unit_grad):
    values = raw.astype(jnp.float32)
    inner = jnp.sum(values * unit_grad, axis=-1, keepdims=True)
    return inv * unit_grad - inv * inv * inv * values * inner


def back_rows(raw, inv, unit_grad):
    return raw_grad(raw, inv, unit_grad).astype(jnp.bfloat16)


def transposed(weight, other):
    return lax.dot_general(
        weight, other, (((0,), (0,)), ((), ())), preferred_element_type=jnp.float32
    )


def plain_weight(dots, scale, bias):
    return (scale * jax.nn.sigmoid(dots * scale + bias)).astype(jnp.bfloat16)


def dot_rows(left, right):
    return lax.dot_general(
        left, right, (((1,), (1,)), ((), ())), preferred_element_type=jnp.float32
    )


def cross_weight(scale_ref, bias_ref, raw_ref, unit_ref):
    other = unit_rows(raw_ref[...])[0]
    dots = dot_rows(unit_ref[...], other)
    return (other, dots, plain_weight(dots, scale_ref[0], bias_ref[0]))


def text_side(scale_ref, bias_ref, raw_ref, unit_ref, total_ref, text_ref, inv_ref, out_ref):
    other, _, weight = cross_weight(scale_ref, bias_ref, raw_ref, unit_ref)
    grad = total_ref[...] + jnp.dot(weight, other, preferred_element_type=jnp.float32)
    out_ref[...] = raw_grad(text_ref[...], inv_ref[...], grad)


def text_last(
    scale_ref, bias_ref, raw_ref, unit_ref, base_ref, text_ref, inv_ref, out_ref, done, sems
):
    other, dots, weight = cross_weight(scale_ref, bias_ref, raw_ref, unit_ref)
    inv = inv_ref[...]
    inner = jnp.sum(weight.astype(jnp.float32) * dots, axis=1, keepdims=True)
    along = inv * inv * inner
    weight = (weight.astype(jnp.float32) * inv).astype(jnp.bfloat16)
    copies = []
    for index, at in enumerate(range(0, done.shape[0], STEP)):
        rows = pl.ds(at, STEP)
        part = jnp.dot(weight[at : at + STEP], other, preferred_element_type=jnp.float32)
        values = text_ref[rows, :].astype(jnp.float32)
        done[rows, :] = (
            base_ref[rows, :] + part - along[at : at + STEP] * values
        ).astype(jnp.bfloat16)
        copies.append(
            pltpu.make_async_copy(done.at[rows, :], out_ref.at[rows, :], sems.at[index])
        )
        copies[-1].start()
    for copy in copies:
        copy.wait()


def call(kernel, out, out_specs, scratch, rows, width, *args):
    smem = pl.BlockSpec(memory_space=pltpu.SMEM)
    vmem = pl.BlockSpec(memory_space=pltpu.VMEM)
    return pl.pallas_call(
        kernel,
        out_shape=out,
        in_specs=[smem, smem] + [vmem] * (len(args) - 2),
        out_specs=out_specs,
        scratch_shapes=scratch,
        compiler_params=pltpu.CompilerParams(vmem_limit_bytes=40 * 1024 * 1024),
        cost_estimate=pl.CostEstimate(
            flops=4 * rows * rows * width,
            bytes_accessed=12 * rows * width,
            transcendentals=2 * rows * rows,
        ),
    )(*args)


def per_device(images, texts, labels, logit_scale, logit_bias):
    rows_per, width = images.shape
    scale = logit_scale[0]
    bias = logit_bias[0]
    col_text = from_partner(texts, "col")
    row_text = from_partner(texts, "row")
    image_unit, image_inv = unit_rows(images)
    col_image = from_partner(images, "col")
    row_image = from_partner(images, "row")
    text_unit, text_inv = unit_rows(texts)
    column_ids = jnp.arange(rows_per, dtype=jnp.int32)
    own_sign = jnp.where(labels[0][:, None] == column_ids[None, :], 1.0, -1.0).astype(jnp.float32)
    loss_own, weight_own = score_block(image_unit, text_unit, scale, bias, own_sign)
    text_total = transposed(weight_own, image_unit)

    col_unit, _ = unit_rows(col_text)
    loss_col, weight_col = score_block(image_unit, col_unit, scale, bias, -1.0)
    loss_col, row_text = lax.optimization_barrier((loss_col, row_text))
    row_unit, _ = unit_rows(row_text)
    loss_row, weight_row = score_block(image_unit, row_unit, scale, bias, -1.0)
    image_unit_grad = (
        jnp.dot(weight_own, text_unit, preferred_element_type=jnp.float32)
        + jnp.dot(weight_col, col_unit, preferred_element_type=jnp.float32)
        + jnp.dot(weight_row, row_unit, preferred_element_type=jnp.float32)
    )
    row_loss = (loss_own + loss_row + loss_col) / (3.0 * rows_per)
    image_grad = back_rows(images, image_inv, image_unit_grad)

    vmem = pl.BlockSpec(memory_space=pltpu.VMEM)
    wide = jax.ShapeDtypeStruct((rows_per, width), jnp.float32)
    half = jax.ShapeDtypeStruct((rows_per, width), jnp.bfloat16)
    image_grad, text_total = lax.optimization_barrier((image_grad, text_total))
    text_total = call(
        text_side, wide, vmem, [], rows_per, width,
        logit_scale, logit_bias, col_image, text_unit, text_total, texts, text_inv,
    )
    text_grad = call(
        text_last, half, pl.BlockSpec(memory_space=pl.ANY),
        [pltpu.VMEM((rows_per, width), jnp.bfloat16), pltpu.SemaphoreType.DMA((rows_per // STEP,))],
        rows_per, width,
        logit_scale, logit_bias, row_image, text_unit, text_total, texts, text_inv,
    )
    return (row_loss, image_grad, text_grad)


def solution(mesh):
    placed = (P(("row", "col"), None), P(("row", "col"), None), P(("row", "col"), None), P(), P())
    return jax.shard_map(
        per_device,
        mesh=mesh,
        in_specs=placed,
        out_specs=(P(("row", "col")), P(("row", "col"), None), P(("row", "col"), None)),
        check_vma=False,
    )
```
